256 devices in a mesh: expert: 8 (over y, x_lo), dp: 32 (over x_hi, z, core).
Axes of the slice: x: 4 (x_hi: 2, x_lo: 2; x = x_hi * 2 + x_lo), y: 4, z: 8, core: 2. Of those that a mesh axis runs over, the one named last changes fastest.
Arguments:
- tokens: bfloat16 [4096, 3072], P(('expert', 'dp')), may hold values from -6 to 6
- cotangent: bfloat16 [4096, 3072], P(('expert', 'dp')), may hold values from -6 to 6
- experts: int32 [4096, 2], P(('expert', 'dp')), may hold values from 0 to 7, all different within a row; in each aligned block of 16 rows (0 to 15, 16 to 31, ...) at most 8 rows name the same one
- gate_weights: float32 [4096, 2], P(('expert', 'dp')), may hold values from 0.1 to 1
- w_up: bfloat16 [8, 3072, 8192], P('expert', None, 'dp'), may hold values from -0.109375 to 0.109375
- master: float32 [8, 8192, 3072], P(None, 'dp', 'expert'), may hold values from -6 to 6
- moment_one: bfloat16 [8, 8192, 3072], P(None, 'dp', 'expert'), may hold values from -18 to 18
- moment_two: bfloat16 [8, 8192, 3072], P(None, 'dp', 'expert'), may hold values from 10 to 100
Outputs:
- new_master: float32 [8, 8192, 3072], P('expert', 'dp')
The draws below stay inside these ranges and needn't reach their ends.
Inputs may be any that keep to these rules, and one draw needn't show every extreme that they name: Each token names two different experts; the tokens of one device name any expert at most 8 times, a bound that some block reaches.
All inputs are finite; a program needn't handle non-finite values.
Results may differ from the reference program's by a relative error of at most 0.0003.
Values may be sent and summed in bfloat16 or wider, within the bound.
A program may use at most 128 MiB of HBM per device.

```python
import math
import jax
import jax.numpy as jnp
import numpy as np
from jax import lax

D = 3072
F = 8192
E = 8
TOK_DEV = 16
CAP = 8
TOKENS = 4096
DEVICES = 256


def steps_of(rng, extent, pieces, least, largest):
    gain = 1.0
    for dim, blocks in pieces:
        steps = jax.random.uniform(jax.random.fold_in(jax.random.fold_in(rng, 6), dim), (blocks,), jnp.float32, least / len(pieces), largest / len(pieces))
        gain = gain * jnp.repeat(jnp.exp(steps), extent[dim] // blocks).reshape((-1,) + (1,) * (len(extent) - 1 - dim))
    return gain


def routed_block(key, own, number, rows, amount, top, limit, slope):
    sequence = jax.random.permutation(key, amount)
    packed, usual = shares(amount, rows * top, limit, slope, True), shares(amount, rows * top, limit, slope, False)
    places = jnp.arange(amount)

    def named(sizes, offset_by):
        used = int((sizes > 0).sum())
        fixed = max(1, used // 4)
        moved = fixed + (places - fixed + offset_by * (used - fixed)) % max(1, amount - fixed)
        return jnp.zeros((amount,), jnp.int32).at[sequence[jnp.where(places < fixed, places, moved)]].set(jnp.asarray(sizes, jnp.int32))

    sizes = jnp.where(number % 4 == 0, named(packed, number // 4), named(usual, number - number // 4 - 1))
    mixed = jax.random.permutation(jax.random.fold_in(own, 3), amount)
    donor, sink = mixed[0:amount // 2 * 2:2], mixed[1:amount // 2 * 2:2]
    room = jnp.minimum(sizes[donor] - 1, limit - sizes[sink]) // 2
    room = jnp.where((donor == sequence[0]) | (sink == sequence[0]) | (sizes[sink] == 0), 0, jnp.maximum(room, 0))
    moved = jax.random.randint(jax.random.fold_in(own, 4), (amount // 2,), 0, 1 << 20) % (room + 1)
    sizes = sizes.at[donor].add(-moved).at[sink].add(moved)
    items = jnp.searchsorted(jnp.cumsum(sizes), jnp.arange(rows * top), side="right").astype(jnp.int32)
    grid = items.reshape(top, rows).T
    grid = grid[jax.random.permutation(jax.random.fold_in(own, 1), rows)]
    offset_by = jax.random.randint(jax.random.fold_in(own, 2), (rows, 1), 0, top)
    return jnp.take_along_axis(grid, (jnp.arange(top)[None, :] + offset_by) % top, axis=1)


def shares(amount, total, most, slope, full):
    weights = [(1 << 20) // math.isqrt(standing ** slope) + 1 for standing in range(1, amount + 1)]
    largest = most if full else min(most, max(-(-total // amount), total * weights[0] // sum(weights)))
    least = 1 if total - largest >= amount - 1 else 0
    holding, surplus = [largest] + [least] * (amount - 1), total - largest - least * (amount - 1)
    while surplus > 0:
        candidates = [i for i in range(1, amount) if holding[i] < largest] or [i for i in range(1, amount) if holding[i] < most]
        whole, budget = sum([weights[i] for i in candidates]), surplus
        for i in candidates:
            addition = min(most - holding[i], max(1, budget * weights[i] // whole), surplus)
            holding[i] = holding[i] + addition
            surplus = surplus - addition
    return np.array(holding)


def scatter_about(own_key, shape, deviation, most, pieces=(), kind=jnp.bfloat16):
    array = deviation * jax.random.normal(own_key, shape, jnp.float32)
    if pieces:
        array = array * steps_of(own_key, shape, pieces, -0.22, 0.18)
    return jnp.clip(array, -most, most).astype(kind)


def setup_inputs(seed: int = 0) -> dict:
    splits = jax.random.split(jax.random.key(seed), 9)
    tokens = scatter_about(splits[0], (TOKENS, D), 1.0, 6.0, ((0, 256),))
    cotangent = scatter_about(splits[1], (TOKENS, D), 1.0, 6.0, ((0, 256),))
    experts_keys = jax.random.split(jax.random.fold_in(splits[2], 1), TOKENS // TOK_DEV)
    experts_turns = jax.random.permutation(jax.random.fold_in(splits[2], 3), TOKENS // TOK_DEV)
    experts = jax.vmap(lambda own, number: routed_block(jax.random.fold_in(splits[2], 2), own, number, TOK_DEV, E, 2, CAP, 2))(experts_keys, experts_turns).reshape((TOKENS, 2))
    gate_weights = jnp.clip(0.1 + 0.9 * jax.random.uniform(splits[3], (TOKENS, 2), jnp.float32) ** steps_of(splits[3], (TOKENS, 2), ((0, 256),), -0.2, 0.2), 0.1, 1.0)
    w_up = scatter_about(splits[4], (E, D, F), D ** -0.5, 0.109375, ((0, 8), (2, 32)))
    master = scatter_about(splits[5], (E, F, D), 1.0, 6.0, ((1, 32), (2, 8)), jnp.float32)
    moment_one = scatter_about(splits[6], (E, F, D), 3.0, 18.0, ((1, 32), (2, 8)))
    moment_two = jnp.clip(jnp.exp(math.log(100.0) - 2.3025851 * jax.random.uniform(splits[7], (E, F, D), jnp.float32) ** steps_of(splits[7], (E, F, D), ((1, 32), (2, 8)), -0.2, 0.2)), 10.0, 100.0).astype(jnp.bfloat16)
    return dict(tokens=tokens, cotangent=cotangent, experts=experts, gate_weights=gate_weights, w_up=w_up, master=master, moment_one=moment_one, moment_two=moment_two)


beta_one = 0.9
beta_two = 0.95
corr_one = 1.0 - (0.9 ** 50) ** 2
corr_two = 1.0 - (0.95 ** 50) ** 2
learn_rate = 0.2
weight_decay = 0.1
epsilon = 1e-08

def reference(tokens, cotangent, experts, gate_weights, w_up, master, moment_one, moment_two):
    row_count = DEVICES * CAP

    def per_expert(expert_index):
        matched = experts == expert_index
        weight = lax.optimization_barrier(jnp.sum(jnp.where(matched, gate_weights, jnp.float32(0.0)), axis=1))
        chosen = jnp.any(matched, axis=1)
        sort_key = jnp.where(chosen, 0, 1).astype(jnp.int32)
        picked = jnp.argsort(sort_key, stable=True)[:row_count].astype(jnp.int32)
        is_live = chosen[picked]
        scaled = (cotangent[picked].astype(jnp.float32) * weight[picked][:, None]).astype(jnp.bfloat16)
        scaled = jnp.where(is_live[:, None], scaled, jnp.zeros_like(scaled))
        hidden = jax.nn.silu(jnp.dot(tokens[picked], w_up[expert_index], preferred_element_type=jnp.float32)).astype(jnp.bfloat16)
        return lax.dot_general(hidden, scaled, (((0,), (0,)), ((), ())), preferred_element_type=jnp.float32)
    gradient = lax.map(per_expert, jnp.arange(E, dtype=jnp.int32))
    first = beta_one * moment_one.astype(jnp.float32) + (1.0 - beta_one) * gradient
    second = beta_two * moment_two.astype(jnp.float32) + (1.0 - beta_two) * gradient * gradient
    update = first / corr_one / (jnp.sqrt(second / corr_two) + epsilon)
    return master - learn_rate * (update + weight_decay * master)
```

```python
import functools

import jax
import jax.numpy as jnp
from jax import lax
from jax.experimental import pallas as pl
from jax.experimental.pallas import tpu as pltpu
from jax.sharding import PartitionSpec as P

CAP = 8
MESH = pl.DeviceIdType.MESH
FACES = 2
CORES = 2
PIECE = 2 * CAP
COLS = 512

beta_one = 0.9
beta_two = 0.95
corr_one = 1.0 - (0.9**50) ** 2
corr_two = 1.0 - (0.95**50) ** 2
learn_rate = 0.2
weight_decay = 0.1
epsilon = 1e-08


def adam_update(master, moment_one, moment_two, gradient):
    first = beta_one * moment_one.astype(jnp.float32) + (1.0 - beta_one) * gradient
    second = beta_two * moment_two.astype(jnp.float32) + (1.0 - beta_two) * gradient * gradient
    update = first / corr_one / (jnp.sqrt(second / corr_two) + epsilon)
    return master - learn_rate * (update + weight_decay * master)


def kernel(
    E,
    Z,
    experts_ref,
    gates_ref,
    tokens_ref,
    cotangent_ref,
    up_ref,
    master_ref,
    one_ref,
    two_ref,
    grad_ref,
    out_master,
    out_one,
    out_two,
    send,
    buf,
    wbuf,
    acts,
    acc,
    give,
    take,
    disp_s,
    disp_r,
    ring_s,
    ring_r,
    state_s,
    state_r,
    up_s,
    up_r,
    tail_s,
    tail_r,
    local_sem,
):
    e = lax.axis_index("expert")
    d = lax.axis_index("dp")
    c = lax.rem(d, CORES)
    z = lax.rem(lax.div(d, CORES), Z)
    xh = lax.div(d, CORES * Z)
    unit = E * PIECE
    half = Z // 2
    D = tokens_ref.shape[1]
    F = up_ref.shape[1]
    width = D // E

    def dp_of(face, layer, core):
        return (face * Z + layer) * CORES + core

    other_face = dp_of(1 - xh, z, c)
    sibling = dp_of(xh, z, 1 - c)
    ahead = dp_of(xh, lax.rem(z + 1, Z), c)
    behind = dp_of(xh, lax.rem(z + Z - 1, Z), c)

    def peer(k):
        return lax.rem(e + k, E)

    barrier = pltpu.get_barrier_semaphore()
    greet = [(peer(k), d) for k in range(1, E)] + [(peer(k), other_face) for k in range(E)]
    greet += [(e, ahead), (e, behind), (e, sibling)]
    for who in greet:
        pl.semaphore_signal(barrier, inc=1, device_id=who, device_id_type=MESH)

    own_up = pltpu.make_async_copy(up_ref, wbuf.at[c], local_sem.at[0])
    own_up.start()

    T = tokens_ref.shape[0]
    row = lax.broadcasted_iota(jnp.int32, (unit, T), 0)
    expert_of = lax.div(row, PIECE)
    slot = lax.rem(row, PIECE)
    is_scaled = slot >= CAP
    slot = lax.rem(slot, CAP)
    first_choice = experts_ref[0:1, :] == expert_of
    second_choice = experts_ref[1:2, :] == expert_of
    named = jnp.logical_or(first_choice, second_choice)
    earlier = lax.broadcasted_iota(jnp.int32, (T, T), 0) < lax.broadcasted_iota(jnp.int32, (T, T), 1)
    place = jnp.dot(
        jnp.where(named, 1.0, 0.0).astype(jnp.bfloat16),
        jnp.where(earlier, 1.0, 0.0).astype(jnp.bfloat16),
        preferred_element_type=jnp.float32,
    )
    hit = jnp.logical_and(named, place == slot.astype(jnp.float32))
    pick_token = jnp.where(jnp.logical_and(hit, jnp.logical_not(is_scaled)), 1.0, 0.0).astype(jnp.bfloat16)
    scaled_hit = jnp.where(jnp.logical_and(hit, is_scaled), 1.0, 0.0)
    pick_scaled = scaled_hit.astype(jnp.bfloat16)
    gate = jnp.where(first_choice, gates_ref[0:1, :], 0.0) + jnp.where(second_choice, gates_ref[1:2, :], 0.0)
    gate = jnp.sum(gate * scaled_hit, axis=1, keepdims=True)

    @pl.loop(0, D // COLS)
    def _(j):
        cols = pl.ds(pl.multiple_of(j * COLS, COLS), COLS)
        rows_token = jnp.dot(pick_token, tokens_ref[:, cols], preferred_element_type=jnp.float32)
        rows_scaled = jnp.dot(pick_scaled, cotangent_ref[:, cols], preferred_element_type=jnp.float32)
        send[:, cols] = (rows_token + rows_scaled * gate).astype(jnp.bfloat16)

    pl.semaphore_wait(barrier, len(greet))

    def piece_of(k):
        return send.at[pl.ds(pl.multiple_of(peer(k) * PIECE, PIECE), PIECE)]

    def landing(stream):
        return buf.at[0, pl.ds(pl.multiple_of(stream * unit + e * PIECE, PIECE), PIECE)]

    dispatch = {}
    for stream, where in ((0, d), (1, other_face)):
        for k in range(E):
            if stream == 0 and k == 0:
                continue
            dispatch[stream, k] = pltpu.make_async_remote_copy(
                src_ref=piece_of(k),
                dst_ref=landing(stream),
                send_sem=disp_s.at[stream, k],
                recv_sem=disp_r.at[stream, k],
                device_id=(peer(k), where),
                device_id_type=MESH,
            )
            dispatch[stream, k].start()
    own_piece = pltpu.make_async_copy(piece_of(0), landing(0), local_sem.at[1])
    own_piece.start()
    give_up = pltpu.make_async_remote_copy(
        src_ref=up_ref,
        dst_ref=wbuf.at[c],
        send_sem=up_s,
        recv_sem=up_r,
        device_id=(e, sibling),
        device_id_type=MESH,
    )
    give_up.start()

    def hops(stream, way):
        return half - (stream ^ way)

    def where_is(stream, way, s):
        if s == 0:
            return buf.at[0, pl.ds(stream * unit, unit)]
        if s == half:
            return buf.at[2 * half - 1, pl.ds(stream * unit, unit)]
        return buf.at[2 * s - 1 + stream, pl.ds(way * unit, unit)]

    ring = {}
    for stream in range(2):
        for way, neighbour in ((0, ahead), (1, behind)):
            for s in range(hops(stream, way)):
                ring[stream, way, s] = pltpu.make_async_remote_copy(
                    src_ref=where_is(stream, way, s),
                    dst_ref=where_is(stream, way, s + 1),
                    send_sem=ring_s.at[stream, way, s],
                    recv_sem=ring_r.at[stream, way, s],
                    device_id=(e, neighbour),
                    device_id_type=MESH,
                )

    def forward(stream, way, s):
        if (stream, way, s) in ring:
            ring[stream, way, s].start()

    for stream in range(2):
        for k in range(E):
            if (stream, k) in dispatch:
                dispatch[stream, k].wait_recv()
        if stream == 0:
            own_piece.wait()
        for way in range(2):
            forward(stream, way, 0)

    own_cols = pl.ds(pl.multiple_of(e * width, width), width)
    state, own_state = [], []
    for k in range(1, E):
        for i, (src, dst) in enumerate(((master_ref, out_master), (one_ref, out_one), (two_ref, out_two))):
            state.append(
                pltpu.make_async_remote_copy(
                    src_ref=src.at[peer(k)],
                    dst_ref=dst.at[:, own_cols],
                    send_sem=state_s.at[i, k],
                    recv_sem=state_r.at[i, k],
                    device_id=(peer(k), d),
                    device_id_type=MESH,
                )
            )
            state[-1].start()
    for i, (src, dst) in enumerate(((master_ref, out_master), (one_ref, out_one), (two_ref, out_two))):
        own_state.append(pltpu.make_async_copy(src.at[e], dst.at[:, own_cols], local_sem.at[2 + i]))
        own_state[-1].start()

    own_up.wait()
    give_up.wait_recv()

    batch_rows = 2 * unit

    def hidden(b):
        @pl.loop(0, CORES)
        def _(h):
            up = jnp.dot(buf[b], wbuf[h], preferred_element_type=jnp.float32)
            up = up / (1.0 + jnp.exp(-up))
            up = up.reshape(batch_rows // PIECE, PIECE, F)[:, :CAP]
            up = jnp.concatenate([jnp.zeros_like(up), up], axis=1).reshape(batch_rows, F)
            acts[pl.ds(pl.multiple_of(h * F, F), F), :] = up.T.astype(jnp.bfloat16)

    def product(b, cols):
        return jnp.dot(acts[...], buf[b, :, cols], preferred_element_type=jnp.float32)

    def compute(b):
        hidden(b)

        @pl.loop(0, D // COLS)
        def _(j):
            cols = pl.ds(pl.multiple_of(j * COLS, COLS), COLS)
            if b == 0:
                acc[:, cols] = product(b, cols)
            else:
                acc[:, cols] += product(b, cols)

    compute(0)
    for s in range(1, half):
        for stream in range(2):
            for way in range(2):
                ring[stream, way, s - 1].wait_recv()
                forward(stream, way, s)
            compute(2 * s - 1 + stream)
    last = 2 * half - 1
    ring[0, 0, half - 1].wait_recv()
    ring[1, 1, half - 1].wait_recv()
    hidden(last)

    theirs = pl.ds(pl.multiple_of((1 - c) * F, F), F)
    mine = pl.ds(pl.multiple_of(c * F, F), F)
    tail = []
    for j in range(D // COLS):
        cols = pl.ds(j * COLS, COLS)
        acc[:, cols] += product(last, cols)
        give[j] = acc[theirs, cols].astype(jnp.bfloat16)
        tail.append(
            pltpu.make_async_remote_copy(
                src_ref=give.at[j],
                dst_ref=take.at[j],
                send_sem=tail_s.at[j],
                recv_sem=tail_r.at[j],
                device_id=(e, sibling),
                device_id_type=MESH,
            )
        )
        tail[-1].start()
    for j in range(D // COLS):
        cols = pl.ds(j * COLS, COLS)
        tail[j].wait_recv()
        grad_ref[:, cols] = acc[mine, cols] + take[j].astype(jnp.float32)

    for copy in state:
        copy.wait()
    for copy in own_state:
        copy.wait()
    for copy in list(dispatch.values()) + [give_up] + list(ring.values()) + tail:
        copy.wait_send()


def body(E, Z, tokens, cotangent, experts, gate_weights, w_up, master, moment_one, moment_two):
    D = tokens.shape[1]
    F = w_up.shape[2]
    unit = E * PIECE
    half = Z // 2
    in_vmem = pl.BlockSpec(memory_space=pltpu.VMEM)
    anywhere = pl.BlockSpec(memory_space=pl.ANY)
    grad, far_master, far_one, far_two = pl.pallas_call(
        functools.partial(kernel, E, Z),
        out_shape=(
            jax.ShapeDtypeStruct((F, D), jnp.float32),
            jax.ShapeDtypeStruct((F, D), jnp.float32),
            jax.ShapeDtypeStruct((F, D), jnp.bfloat16),
            jax.ShapeDtypeStruct((F, D), jnp.bfloat16),
        ),
        in_specs=[in_vmem] * 4 + [anywhere] * 4,
        out_specs=(in_vmem, anywhere, anywhere, anywhere),
        scratch_shapes=[
            pltpu.VMEM((unit, D), jnp.bfloat16),
            pltpu.VMEM((Z, 2 * unit, D), jnp.bfloat16),
            pltpu.VMEM((CORES, D, F), jnp.bfloat16),
            pltpu.VMEM((CORES * F, 2 * unit), jnp.bfloat16),
            pltpu.VMEM((CORES * F, D), jnp.float32),
            pltpu.VMEM((D // COLS, F, COLS), jnp.bfloat16),
            pltpu.VMEM((D // COLS, F, COLS), jnp.bfloat16),
            pltpu.SemaphoreType.DMA((2, E)),
            pltpu.SemaphoreType.DMA((2, E)),
            pltpu.SemaphoreType.DMA((2, 2, half)),
            pltpu.SemaphoreType.DMA((2, 2, half)),
            pltpu.SemaphoreType.DMA((3, E)),
            pltpu.SemaphoreType.DMA((3, E)),
            pltpu.SemaphoreType.DMA,
            pltpu.SemaphoreType.DMA,
            pltpu.SemaphoreType.DMA((D // COLS,)),
            pltpu.SemaphoreType.DMA((D // COLS,)),
            pltpu.SemaphoreType.DMA((5,)),
        ],
        compiler_params=pltpu.CompilerParams(
            collective_id=0, has_side_effects=True, vmem_limit_bytes=48 * 1024 * 1024
        ),
    )(experts.T, gate_weights.T, tokens, cotangent, w_up[0], master, moment_one, moment_two)
    return adam_update(far_master, far_one, far_two, grad)[None]


def solution(mesh):
    E = mesh.shape["expert"]
    Z = mesh.shape["dp"] // (FACES * CORES)
    placed = (
        P(("expert", "dp"), None),
        P(("expert", "dp"), None),
        P(("expert", "dp"), None),
        P(("expert", "dp"), None),
        P("expert", None, "dp"),
        P(None, "dp", "expert"),
        P(None, "dp", "expert"),
        P(None, "dp", "expert"),
    )
    return jax.shard_map(
        functools.partial(body, E, Z),
        mesh=mesh,
        in_specs=placed,
        out_specs=P("expert", "dp", None),
        check_vma=False,
    )
```

```python
import functools

import jax
import jax.numpy as jnp
from jax import lax
from jax.experimental import pallas as pl
from jax.experimental.pallas import tpu as pltpu
from jax.sharding import PartitionSpec as P

CAP = 8
MESH = pl.DeviceIdType.MESH
FACES = 2
CORES = 2
NEIGHBOURS = 2
PIECE = 2 * CAP
COLS = 512

beta_one = 0.9
beta_two = 0.95
corr_one = 1.0 - (0.9**50) ** 2
corr_two = 1.0 - (0.95**50) ** 2
learn_rate = 0.2
weight_decay = 0.1
epsilon = 1e-08


def adam_update(master, moment_one, moment_two, gradient):
    first = beta_one * moment_one.astype(jnp.float32) + (1.0 - beta_one) * gradient
    second = beta_two * moment_two.astype(jnp.float32) + (1.0 - beta_two) * gradient * gradient
    update = first / corr_one / (jnp.sqrt(second / corr_two) + epsilon)
    return master - learn_rate * (update + weight_decay * master)


def kernel(
    E,
    Z,
    experts_in,
    gates_in,
    tokens_in,
    cotangent_in,
    up_ref,
    master_ref,
    one_ref,
    two_ref,
    out_ref,
    experts_ref,
    gates_ref,
    tokens_ref,
    cotangent_ref,
    send,
    buf,
    wbuf,
    acts,
    acc,
    give,
    take,
    far_master,
    far_one,
    far_two,
    disp_s,
    disp_r,
    ring_s,
    ring_r,
    face_s,
    face_r,
    state_s,
    state_r,
    up_s,
    up_r,
    tail_s,
    tail_r,
    local_sem,
    out_sem,
):
    e = lax.axis_index("expert")
    d = lax.axis_index("dp")
    c = lax.rem(d, CORES)
    z = lax.rem(lax.div(d, CORES), Z)
    xh = lax.div(d, CORES * Z)
    unit = E * PIECE
    part = unit // 2
    half = Z // 2
    D = tokens_ref.shape[1]
    F = up_ref.shape[1]
    width = D // E
    steps = D // COLS

    def dp_of(face, layer, core):
        return (face * Z + layer) * CORES + core

    other_face = dp_of(1 - xh, z, c)
    sibling = dp_of(xh, z, 1 - c)
    ahead = dp_of(xh, lax.rem(z + 1, Z), c)
    behind = dp_of(xh, lax.rem(z + Z - 1, Z), c)

    Y = E // NEIGHBOURS
    offsets = [(0, 0), (0, 1), (1, 0), (Y - 1, 0)]
    offsets += [(dy, dx) for dy in range(Y) for dx in range(NEIGHBOURS) if (dy, dx) not in offsets]
    near = 4

    def peer(k):
        dy, dx = offsets[k]
        y = lax.rem(lax.div(e, NEIGHBOURS) + dy, Y)
        x = lax.rem(lax.rem(e, NEIGHBOURS) + dx, NEIGHBOURS)
        return y * NEIGHBOURS + x

    barrier = pltpu.get_barrier_semaphore()
    greet = [(peer(k), d) for k in range(1, E)] + [(peer(k), other_face) for k in range(E)]
    greet += [(e, ahead), (e, behind), (e, sibling)]
    for who in greet:
        pl.semaphore_signal(barrier, inc=1, device_id=who, device_id_type=MESH)

    loads = [
        pltpu.make_async_copy(src, dst, local_sem.at[5 + i])
        for i, (src, dst) in enumerate(
            (
                (experts_in, experts_ref),
                (gates_in, gates_ref),
                (tokens_in, tokens_ref),
                (cotangent_in, cotangent_ref),
            )
        )
    ]
    for copy in loads:
        copy.start()
    own_up = pltpu.make_async_copy(up_ref, wbuf.at[c], local_sem.at[0])
    own_up.start()
    for copy in loads:
        copy.wait()

    T = tokens_ref.shape[0]
    row = lax.broadcasted_iota(jnp.int32, (unit, T), 0)
    expert_of = lax.div(row, PIECE)
    slot = lax.rem(row, PIECE)
    is_scaled = slot >= CAP
    slot = lax.rem(slot, CAP)
    first_choice = experts_ref[0:1, :] == expert_of
    second_choice = experts_ref[1:2, :] == expert_of
    named = jnp.logical_or(first_choice, second_choice)
    earlier = lax.broadcasted_iota(jnp.int32, (T, T), 0) < lax.broadcasted_iota(jnp.int32, (T, T), 1)
    place = jnp.dot(
        jnp.where(named, 1.0, 0.0).astype(jnp.bfloat16),
        jnp.where(earlier, 1.0, 0.0).astype(jnp.bfloat16),
        preferred_element_type=jnp.float32,
    )
    hit = jnp.logical_and(named, place == slot.astype(jnp.float32))
    pick_token = jnp.where(jnp.logical_and(hit, jnp.logical_not(is_scaled)), 1.0, 0.0).astype(jnp.bfloat16)
    scaled_hit = jnp.where(jnp.logical_and(hit, is_scaled), 1.0, 0.0)
    pick_scaled = scaled_hit.astype(jnp.bfloat16)
    gate = jnp.where(first_choice, gates_ref[0:1, :], 0.0) + jnp.where(second_choice, gates_ref[1:2, :], 0.0)
    gate = jnp.sum(gate * scaled_hit, axis=1, keepdims=True)

    @pl.loop(0, steps)
    def _(j):
        cols = pl.ds(pl.multiple_of(j * COLS, COLS), COLS)
        rows_token = jnp.dot(pick_token, tokens_ref[:, cols], preferred_element_type=jnp.float32)
        rows_scaled = jnp.dot(pick_scaled, cotangent_ref[:, cols], preferred_element_type=jnp.float32)
        send[:, cols] = (rows_token + rows_scaled * gate).astype(jnp.bfloat16)

    pl.semaphore_wait(barrier, len(greet))

    def piece_of(k):
        return send.at[pl.ds(pl.multiple_of(peer(k) * PIECE, PIECE), PIECE)]

    def landing(stream, k):
        return buf.at[0, pl.ds(stream * unit + k * PIECE, PIECE)]

    dispatch = {}
    for stream, where in ((0, d), (1, other_face)):
        for k in range(E):
            if stream or k:
                dispatch[stream, k] = pltpu.make_async_remote_copy(
                    src_ref=piece_of(k),
                    dst_ref=landing(stream, k),
                    send_sem=disp_s.at[stream, k],
                    recv_sem=disp_r.at[stream, k],
                    device_id=(peer(k), where),
                    device_id_type=MESH,
                )
    own_piece = pltpu.make_async_copy(piece_of(0), landing(0, 0), local_sem.at[1])
    own_piece.start()
    for k in range(1, near):
        dispatch[0, k].start()
    give_up = pltpu.make_async_remote_copy(
        src_ref=up_ref,
        dst_ref=wbuf.at[c],
        send_sem=up_s,
        recv_sem=up_r,
        device_id=(e, sibling),
        device_id_type=MESH,
    )

    def lies(stream, way, s, h):
        if s == 0:
            b, at = 0, stream * 2 + h
        elif s == half:
            b, at = half, stream * 2 + h
        elif stream == 0:
            b, at = s, way * 2 + h
        elif s == half - 1:
            b, at = 2 * half - 1, (1 - h) * 2 + way
        else:
            b, at = half + s, way * 2 + h
        return buf.at[b, pl.ds(at * part, part)]

    ring = {}
    for stream in range(2):
        for way, neighbour in ((0, ahead), (1, behind)):
            for s in range(half - stream):
                for h in range(2):
                    if (stream == 0 and s == half - 1 and h != way):
                        continue
                    ring[stream, way, s, h] = pltpu.make_async_remote_copy(
                        src_ref=lies(stream, way, s, h),
                        dst_ref=lies(stream, way, s + 1, h),
                        send_sem=ring_s.at[stream, way, s, h],
                        recv_sem=ring_r.at[stream, way, s, h],
                        device_id=(e, neighbour),
                        device_id_type=MESH,
                    )

    faces = {}
    for i, (way, s, h) in enumerate(((0, half, 0), (1, half, 1))):
        faces[way, s, h] = pltpu.make_async_remote_copy(
            src_ref=lies(0, way, s, h),
            dst_ref=lies(1, way, s, h),
            send_sem=face_s.at[i],
            recv_sem=face_r.at[i],
            device_id=(e, other_face),
            device_id_type=MESH,
        )

    def pass_on(stream, way, s, h):
        if (stream, way, s, h) in ring:
            ring[stream, way, s, h].start()
        if stream == 0 and (way, s, h) in faces:
            faces[way, s, h].start()

    def arrive(stream, s, h):
        for way in range(2):
            if (stream, way, s - 1, h) in ring:
                ring[stream, way, s - 1, h].wait_recv()
                pass_on(stream, way, s, h)

    own_piece.wait()
    for k in range(1, near):
        dispatch[0, k].wait_send()
    for k in range(near, E):
        dispatch[0, k].start()
    for h in range(2):
        for k in range(max(1, h * near), (h + 1) * near):
            dispatch[0, k].wait_recv()
        for way in range(2):
            pass_on(0, way, 0, h)
    give_up.start()
    for k in range(E):
        dispatch[1, k].start()

    own_cols = pl.ds(pl.multiple_of(e * width, width), width)
    state, own_state = [], []
    for k in range(1, E):
        for i, (src, dst) in enumerate(((master_ref, far_master), (one_ref, far_one), (two_ref, far_two))):
            state.append(
                pltpu.make_async_remote_copy(
                    src_ref=src.at[peer(k)],
                    dst_ref=dst.at[:, own_cols],
                    send_sem=state_s.at[i, k],
                    recv_sem=state_r.at[i, k],
                    device_id=(peer(k), d),
                    device_id_type=MESH,
                )
            )
            state[-1].start()
    for i, (src, dst) in enumerate(((master_ref, far_master), (one_ref, far_one), (two_ref, far_two))):
        own_state.append(pltpu.make_async_copy(src.at[e], dst.at[:, own_cols], local_sem.at[2 + i]))
        own_state[-1].start()

    own_up.wait()
    give_up.wait_recv()

    def hidden(b, first, rows):
        @pl.loop(0, CORES)
        def _(h):
            up = jnp.dot(buf[b, first : first + rows], wbuf[h], preferred_element_type=jnp.float32)
            up = up / (1.0 + jnp.exp(-up))
            up = up.reshape(rows // PIECE, PIECE, F)[:, :CAP]
            up = jnp.concatenate([jnp.zeros_like(up), up], axis=1).reshape(rows, F)
            acts[pl.ds(pl.multiple_of(h * F, F), F), :rows] = up.T.astype(jnp.bfloat16)

    def product(b, first, rows, cols):
        return jnp.dot(
            acts[:, :rows], buf[b, first : first + rows, cols], preferred_element_type=jnp.float32
        )

    def compute(b, first=0, rows=2 * unit, fresh=False):
        hidden(b, first, rows)

        @pl.loop(0, steps)
        def _(j):
            cols = pl.ds(pl.multiple_of(j * COLS, COLS), COLS)
            if fresh:
                acc[:, cols] = product(b, first, rows, cols)
            else:
                acc[:, cols] += product(b, first, rows, cols)

    for s in range(1, half):
        for h in range(2):
            arrive(0, s, h)
            if s == half - 1 and h == 0:
                for k in range(E):
                    dispatch[1, k].wait_recv()
                for g in range(2):
                    for way in range(2):
                        pass_on(1, way, 0, g)
        compute(s, fresh=s == 1)
    compute(0)
    for h in range(2):
        arrive(0, half, h)
    for s in range(1, half - 1):
        for h in range(2):
            arrive(1, s, h)
        compute(half + s)
    faces[0, half, 0].wait_recv()
    faces[1, half, 1].wait_recv()
    compute(half)
    last = 2 * half - 1
    arrive(1, half - 1, 1)
    compute(last, 0, unit)
    arrive(1, half - 1, 0)
    hidden(last, unit, unit)

    theirs = pl.ds(pl.multiple_of((1 - c) * F, F), F)
    mine = pl.ds(pl.multiple_of(c * F, F), F)
    tail, outs = [], []
    for j in range(steps):
        cols = pl.ds(j * COLS, COLS)
        acc[:, cols] += product(last, unit, unit, cols)
        give[j] = acc[theirs, cols].astype(jnp.bfloat16)
        tail.append(
            pltpu.make_async_remote_copy(
                src_ref=give.at[j],
                dst_ref=take.at[j],
                send_sem=tail_s.at[j],
                recv_sem=tail_r.at[j],
                device_id=(e, sibling),
                device_id_type=MESH,
            )
        )
        tail[-1].start()
    for copy in state:
        copy.wait()
    for copy in own_state:
        copy.wait()
    for j in range(steps):
        cols = pl.ds(j * COLS, COLS)
        tail[j].wait_recv()
        gradient = acc[mine, cols] + take[j].astype(jnp.float32)
        acc[mine, cols] = adam_update(far_master[:, cols], far_one[:, cols], far_two[:, cols], gradient)
        outs.append(pltpu.make_async_copy(acc.at[mine, cols], out_ref.at[:, cols], out_sem.at[j]))
        outs[-1].start()
    for k, copy in dispatch.items():
        if k[0] or k[1] >= near:
            copy.wait_send()
    for copy in [give_up] + list(ring.values()) + list(faces.values()) + tail:
        copy.wait_send()
    for copy in outs:
        copy.wait()


def body(E, Z, tokens, cotangent, experts, gate_weights, w_up, master, moment_one, moment_two):
    T, D = tokens.shape
    F = w_up.shape[2]
    unit = E * PIECE
    half = Z // 2
    anywhere = pl.BlockSpec(memory_space=pl.ANY)
    fresh = pl.pallas_call(
        functools.partial(kernel, E, Z),
        out_shape=jax.ShapeDtypeStruct((F, D), jnp.float32),
        in_specs=[anywhere] * 8,
        out_specs=anywhere,
        scratch_shapes=[
            pltpu.VMEM((2, T), jnp.int32),
            pltpu.VMEM((2, T), jnp.float32),
            pltpu.VMEM((T, D), jnp.bfloat16),
            pltpu.VMEM((T, D), jnp.bfloat16),
            pltpu.VMEM((unit, D), jnp.bfloat16),
            pltpu.VMEM((Z, 2 * unit, D), jnp.bfloat16),
            pltpu.VMEM((CORES, D, F), jnp.bfloat16),
            pltpu.VMEM((CORES * F, 2 * unit), jnp.bfloat16),
            pltpu.VMEM((CORES * F, D), jnp.float32),
            pltpu.VMEM((D // COLS, F, COLS), jnp.bfloat16),
            pltpu.VMEM((D // COLS, F, COLS), jnp.bfloat16),
            pltpu.VMEM((F, D), jnp.float32),
            pltpu.VMEM((F, D), jnp.bfloat16),
            pltpu.VMEM((F, D), jnp.bfloat16),
            pltpu.SemaphoreType.DMA((2, E)),
            pltpu.SemaphoreType.DMA((2, E)),
            pltpu.SemaphoreType.DMA((2, 2, half, 2)),
            pltpu.SemaphoreType.DMA((2, 2, half, 2)),
            pltpu.SemaphoreType.DMA((4,)),
            pltpu.SemaphoreType.DMA((4,)),
            pltpu.SemaphoreType.DMA((3, E)),
            pltpu.SemaphoreType.DMA((3, E)),
            pltpu.SemaphoreType.DMA,
            pltpu.SemaphoreType.DMA,
            pltpu.SemaphoreType.DMA((D // COLS,)),
            pltpu.SemaphoreType.DMA((D // COLS,)),
            pltpu.SemaphoreType.DMA((9,)),
            pltpu.SemaphoreType.DMA((D // COLS,)),
        ],
        compiler_params=pltpu.CompilerParams(
            collective_id=0, has_side_effects=True, vmem_limit_bytes=60 * 1024 * 1024
        ),
    )(experts.T, gate_weights.T, tokens, cotangent, w_up[0], master, moment_one, moment_two)
    return fresh[None]


def solution(mesh):
    E = mesh.shape["expert"]
    Z = mesh.shape["dp"] // (FACES * CORES)
    placed = (
        P(("expert", "dp"), None),
        P(("expert", "dp"), None),
        P(("expert", "dp"), None),
        P(("expert", "dp"), None),
        P("expert", None, "dp"),
        P(None, "dp", "expert"),
        P(None, "dp", "expert"),
        P(None, "dp", "expert"),
    )
    return jax.shard_map(
        functools.partial(body, E, Z),
        mesh=mesh,
        in_specs=placed,
        out_specs=P("expert", "dp", None),
        check_vma=False,
    )
```

```python
import functools

import jax
import jax.numpy as jnp
from jax import lax
from jax.experimental import pallas as pl
from jax.experimental.pallas import tpu as pltpu
from jax.sharding import PartitionSpec as P

CAP = 8
MESH = pl.DeviceIdType.MESH
FACES = 2
CORES = 2
NEIGHBOURS = 2
PIECE = 2 * CAP
COLS = 512
SETTLE = 8

beta_one = 0.9
beta_two = 0.95
corr_one = 1.0 - (0.9**50) ** 2
corr_two = 1.0 - (0.95**50) ** 2
learn_rate = 0.2
weight_decay = 0.1
epsilon = 1e-08


def adam_update(master, moment_one, moment_two, gradient):
    first = beta_one * moment_one.astype(jnp.float32) + (1.0 - beta_one) * gradient
    second = beta_two * moment_two.astype(jnp.float32) + (1.0 - beta_two) * gradient * gradient
    update = first / corr_one / (jnp.sqrt(second / corr_two) + epsilon)
    return master - learn_rate * (update + weight_decay * master)


def kernel(
    E,
    Z,
    experts_in,
    gates_in,
    tokens_in,
    cotangent_in,
    up_ref,
    master_ref,
    one_ref,
    two_ref,
    out_ref,
    experts_ref,
    gates_ref,
    tokens_ref,
    cotangent_ref,
    send,
    buf,
    wbuf,
    acts,
    acc,
    give,
    take,
    extra,
    far_master,
    far_one,
    far_two,
    disp_s,
    disp_r,
    ring_s,
    ring_r,
    face_s,
    face_r,
    state_s,
    state_r,
    up_s,
    up_r,
    tail_s,
    tail_r,
    share_s,
    share_r,
    early_s,
    early_r,
    local_sem,
    out_sem,
):
    e = lax.axis_index("expert")
    d = lax.axis_index("dp")
    c = lax.rem(d, CORES)
    z = lax.rem(lax.div(d, CORES), Z)
    xh = lax.div(d, CORES * Z)
    unit = E * PIECE
    part = unit // 2
    half = Z // 2
    D = tokens_ref.shape[1]
    F = up_ref.shape[1]
    width = D // E
    steps = D // COLS

    def dp_of(face, layer, core):
        return (face * Z + layer) * CORES + core

    other_face = dp_of(1 - xh, z, c)
    sibling = dp_of(xh, z, 1 - c)
    ahead = dp_of(xh, lax.rem(z + 1, Z), c)
    behind = dp_of(xh, lax.rem(z + Z - 1, Z), c)

    Y = E // NEIGHBOURS
    offsets = [(0, 0), (0, 1), (1, 0), (Y - 1, 0)]
    offsets += [(dy, dx) for dy in range(Y) for dx in range(NEIGHBOURS) if (dy, dx) not in offsets]
    near = 4

    def peer(k):
        dy, dx = offsets[k]
        y = lax.rem(lax.div(e, NEIGHBOURS) + dy, Y)
        x = lax.rem(lax.rem(e, NEIGHBOURS) + dx, NEIGHBOURS)
        return y * NEIGHBOURS + x

    barrier = pltpu.get_barrier_semaphore()
    greet = [(peer(k), d) for k in range(1, E)] + [(peer(k), other_face) for k in range(E)]
    greet += [(e, ahead), (e, behind), (e, sibling)]
    for who in greet:
        pl.semaphore_signal(barrier, inc=1, device_id=who, device_id_type=MESH)

    loads = [
        pltpu.make_async_copy(src, dst, local_sem.at[5 + i])
        for i, (src, dst) in enumerate(
            (
                (experts_in, experts_ref),
                (gates_in, gates_ref),
                (tokens_in, tokens_ref),
                (cotangent_in, cotangent_ref),
            )
        )
    ]
    for copy in loads:
        copy.start()
    own_up = pltpu.make_async_copy(up_ref, wbuf.at[c], local_sem.at[0])
    own_up.start()
    for copy in loads:
        copy.wait()

    T = tokens_ref.shape[0]
    row = lax.broadcasted_iota(jnp.int32, (unit, T), 0)
    expert_of = lax.div(row, PIECE)
    slot = lax.rem(row, PIECE)
    is_scaled = slot >= CAP
    slot = lax.rem(slot, CAP)
    first_choice = experts_ref[0:1, :] == expert_of
    second_choice = experts_ref[1:2, :] == expert_of
    named = jnp.logical_or(first_choice, second_choice)
    earlier = lax.broadcasted_iota(jnp.int32, (T, T), 0) < lax.broadcasted_iota(jnp.int32, (T, T), 1)
    place = jnp.dot(
        jnp.where(named, 1.0, 0.0).astype(jnp.bfloat16),
        jnp.where(earlier, 1.0, 0.0).astype(jnp.bfloat16),
        preferred_element_type=jnp.float32,
    )
    hit = jnp.logical_and(named, place == slot.astype(jnp.float32))
    pick_token = jnp.where(jnp.logical_and(hit, jnp.logical_not(is_scaled)), 1.0, 0.0).astype(jnp.bfloat16)
    scaled_hit = jnp.where(jnp.logical_and(hit, is_scaled), 1.0, 0.0)
    pick_scaled = scaled_hit.astype(jnp.bfloat16)
    gate = jnp.where(first_choice, gates_ref[0:1, :], 0.0) + jnp.where(second_choice, gates_ref[1:2, :], 0.0)
    gate = jnp.sum(gate * scaled_hit, axis=1, keepdims=True)

    @pl.loop(0, steps)
    def _(j):
        cols = pl.ds(pl.multiple_of(j * COLS, COLS), COLS)
        rows_token = jnp.dot(pick_token, tokens_ref[:, cols], preferred_element_type=jnp.float32)
        rows_scaled = jnp.dot(pick_scaled, cotangent_ref[:, cols], preferred_element_type=jnp.float32)
        send[:, cols] = (rows_token + rows_scaled * gate).astype(jnp.bfloat16)

    pl.semaphore_wait(barrier, len(greet))

    def piece_of(k):
        return send.at[pl.ds(pl.multiple_of(peer(k) * PIECE, PIECE), PIECE)]

    def landing(stream, k):
        return buf.at[0, pl.ds(stream * unit + k * PIECE, PIECE)]

    dispatch = {}
    for stream, where in ((0, d), (1, other_face)):
        for k in range(E):
            if stream or k:
                dispatch[stream, k] = pltpu.make_async_remote_copy(
                    src_ref=piece_of(k),
                    dst_ref=landing(stream, k),
                    send_sem=disp_s.at[stream, k],
                    recv_sem=disp_r.at[stream, k],
                    device_id=(peer(k), where),
                    device_id_type=MESH,
                )
    early = [
        pltpu.make_async_remote_copy(
            src_ref=piece_of(0),
            dst_ref=buf.at[1, pl.ds(way * unit, PIECE)],
            send_sem=early_s.at[way],
            recv_sem=early_r.at[way],
            device_id=(e, neighbour),
            device_id_type=MESH,
        )
        for way, neighbour in ((0, ahead), (1, behind))
    ]
    for copy in early:
        copy.start()
    own_piece = pltpu.make_async_copy(piece_of(0), landing(0, 0), local_sem.at[1])
    own_piece.start()
    for k in range(1, near):
        dispatch[0, k].start()
    give_up = pltpu.make_async_remote_copy(
        src_ref=up_ref,
        dst_ref=wbuf.at[c],
        send_sem=up_s,
        recv_sem=up_r,
        device_id=(e, sibling),
        device_id_type=MESH,
    )

    def lies(stream, way, s, h, skip=0):
        if s == 0:
            b, at = 0, stream * 2 + h
        elif s == half:
            b, at = half, stream * 2 + h
        elif stream == 0:
            b, at = s, way * 2 + h
        elif s == half - 1:
            b, at = 2 * half - 1, (1 - h) * 2 + way
        else:
            b, at = half + s, way * 2 + h
        return buf.at[b, pl.ds(at * part + skip, part - skip)]

    ring = {}
    for stream in range(2):
        for way, neighbour in ((0, ahead), (1, behind)):
            for s in range(half - stream):
                for h in range(2):
                    if (stream == 0 and s == half - 1 and h != way):
                        continue
                    skip = PIECE if (stream, s, h) == (0, 0, 0) else 0
                    ring[stream, way, s, h] = pltpu.make_async_remote_copy(
                        src_ref=lies(stream, way, s, h, skip),
                        dst_ref=lies(stream, way, s + 1, h, skip),
                        send_sem=ring_s.at[stream, way, s, h],
                        recv_sem=ring_r.at[stream, way, s, h],
                        device_id=(e, neighbour),
                        device_id_type=MESH,
                    )

    faces = {}
    for i, (way, s, h) in enumerate(((0, half, 0), (1, half, 1))):
        faces[way, s, h] = pltpu.make_async_remote_copy(
            src_ref=lies(0, way, s, h),
            dst_ref=lies(1, way, s, h),
            send_sem=face_s.at[i],
            recv_sem=face_r.at[i],
            device_id=(e, other_face),
            device_id_type=MESH,
        )

    def pass_on(stream, way, s, h):
        if (stream, way, s, h) in ring:
            ring[stream, way, s, h].start()
        if stream == 0 and (way, s, h) in faces:
            faces[way, s, h].start()

    def arrive(stream, s, h):
        for way in range(2):
            if (stream, way, s - 1, h) in ring:
                ring[stream, way, s - 1, h].wait_recv()
                if (stream, s, h) == (0, 1, 0):
                    early[way].wait_recv()
                pass_on(stream, way, s, h)

    own_piece.wait()
    for k in range(1, near):
        dispatch[0, k].wait_send()
    for k in range(near, E):
        dispatch[0, k].start()
    for h in range(2):
        for k in range(max(1, h * near), (h + 1) * near):
            dispatch[0, k].wait_recv()
        for way in range(2):
            pass_on(0, way, 0, h)
    give_up.start()
    for k in range(E):
        dispatch[1, k].start()

    own_cols = pl.ds(pl.multiple_of(e * width, width), width)
    state, own_state = [], []
    for k in range(1, E):
        for i, (src, dst) in enumerate(((master_ref, far_master), (one_ref, far_one), (two_ref, far_two))):
            state.append(
                pltpu.make_async_remote_copy(
                    src_ref=src.at[peer(k)],
                    dst_ref=dst.at[:, own_cols],
                    send_sem=state_s.at[i, k],
                    recv_sem=state_r.at[i, k],
                    device_id=(peer(k), d),
                    device_id_type=MESH,
                )
            )
            state[-1].start()
    for i, (src, dst) in enumerate(((master_ref, far_master), (one_ref, far_one), (two_ref, far_two))):
        own_state.append(pltpu.make_async_copy(src.at[e], dst.at[:, own_cols], local_sem.at[2 + i]))
        own_state[-1].start()

    own_up.wait()
    give_up.wait_recv()

    def activation(rows_of, weight):
        rows = rows_of.shape[0]
        up = jnp.dot(rows_of, weight, preferred_element_type=jnp.float32)
        up = up / (1.0 + jnp.exp(-up))
        up = up.reshape(rows // PIECE, PIECE, F)[:, :CAP]
        up = jnp.concatenate([jnp.zeros_like(up), up], axis=1).reshape(rows, F)
        return up.T.astype(jnp.bfloat16)

    def hidden(b, first, rows):
        @pl.loop(0, CORES)
        def _(h):
            acts[pl.ds(pl.multiple_of(h * F, F), F), :rows] = activation(buf[b, first : first + rows], wbuf[h])

    def product(b, first, rows, cols):
        return jnp.dot(
            acts[:, :rows], buf[b, first : first + rows, cols], preferred_element_type=jnp.float32
        )

    def compute(b, first=0, rows=2 * unit, fresh=False):
        hidden(b, first, rows)

        @pl.loop(0, steps)
        def _(j):
            cols = pl.ds(pl.multiple_of(j * COLS, COLS), COLS)
            if fresh:
                acc[:, cols] = product(b, first, rows, cols)
            else:
                acc[:, cols] += product(b, first, rows, cols)

    for s in range(1, half):
        for h in range(2):
            arrive(0, s, h)
            if s == half - 1 and h == 0:
                for k in range(E):
                    dispatch[1, k].wait_recv()
                for g in range(2):
                    for way in range(2):
                        pass_on(1, way, 0, g)
        compute(s, fresh=s == 1)
    compute(0)
    for h in range(2):
        arrive(0, half, h)
    for s in range(1, half - 1):
        for h in range(2):
            arrive(1, s, h)
        compute(half + s)
    faces[0, half, 0].wait_recv()
    faces[1, half, 1].wait_recv()
    compute(half)

    theirs = pl.ds(pl.multiple_of((1 - c) * F, F), F)
    mine = pl.ds(pl.multiple_of(c * F, F), F)
    tail, outs = [], []
    for j in range(steps):
        give[j] = acc[theirs, pl.ds(j * COLS, COLS)].astype(jnp.bfloat16)
        tail.append(
            pltpu.make_async_remote_copy(
                src_ref=give.at[j],
                dst_ref=take.at[j],
                send_sem=tail_s.at[j],
                recv_sem=tail_r.at[j],
                device_id=(e, sibling),
                device_id_type=MESH,
            )
        )
        tail[-1].start()
    last = 2 * half - 1
    shared = [
        pltpu.make_async_remote_copy(
            src_ref=buf.at[last, pl.ds((1 - h) * unit, unit)],
            dst_ref=extra.at[pl.ds((1 - h) * unit, unit)],
            send_sem=share_s.at[h],
            recv_sem=share_r.at[h],
            device_id=(e, sibling),
            device_id_type=MESH,
        )
        for h in range(2)
    ]

    def both(h, cols):
        first = (1 - h) * unit
        own = jnp.dot(acts[:F, :unit], buf[last, first : first + unit, cols], preferred_element_type=jnp.float32)
        other = jnp.dot(acts[F:, :unit], extra[first : first + unit, cols], preferred_element_type=jnp.float32)
        return own + other

    for j in range(steps):
        tail[j].wait_recv()
        acc[mine, pl.ds(j * COLS, COLS)] += take[j].astype(jnp.float32)
    for h in range(2):
        first = (1 - h) * unit
        arrive(1, half - 1, h)
        shared[h].start()
        acts[:F, :unit] = activation(buf[last, first : first + unit], wbuf[c])
        shared[h].wait_recv()
        acts[F:, :unit] = activation(extra[first : first + unit], wbuf[c])
        if h == 0:
            for j in range(steps):
                cols = pl.ds(j * COLS, COLS)
                acc[mine, cols] += both(h, cols)
            for copy in state:
                copy.wait()
            for copy in own_state:
                copy.wait()
        else:
            for j in range(steps):
                cols = pl.ds(j * COLS, COLS)
                gradient = acc[mine, cols] + both(h, cols)
                acc[mine, cols] = adam_update(far_master[:, cols], far_one[:, cols], far_two[:, cols], gradient)
                outs.append(pltpu.make_async_copy(acc.at[mine, cols], out_ref.at[:, cols], out_sem.at[j]))
                outs[-1].start()
    for k, copy in dispatch.items():
        if k[0] or k[1] >= near:
            copy.wait_send()
    for copy in [give_up] + list(ring.values()) + list(faces.values()) + tail + shared + early:
        copy.wait_send()
    for copy in outs:
        copy.wait()


def settle(pieces, src_ref, dst_ref, held, in_sems, out_sems):
    rows = src_ref.shape[0] // pieces
    coming, going = [], []
    for i in range(pieces):
        at = pl.ds(i * rows, rows)
        coming.append(pltpu.make_async_copy(src_ref.at[at], held.at[at], in_sems.at[i]))
        going.append(pltpu.make_async_copy(held.at[at], dst_ref.at[at], out_sems.at[i]))
        coming[-1].start()
    for i in range(pieces):
        coming[i].wait()
        going[i].start()
    for copy in going:
        copy.wait()


def body(E, Z, tokens, cotangent, experts, gate_weights, w_up, master, moment_one, moment_two):
    T, D = tokens.shape
    F = w_up.shape[2]
    unit = E * PIECE
    half = Z // 2
    anywhere = pl.BlockSpec(memory_space=pl.ANY)
    fresh = pl.pallas_call(
        functools.partial(kernel, E, Z),
        out_shape=jax.ShapeDtypeStruct((F, D), jnp.float32),
        in_specs=[anywhere] * 8,
        out_specs=anywhere,
        scratch_shapes=[
            pltpu.VMEM((2, T), jnp.int32),
            pltpu.VMEM((2, T), jnp.float32),
            pltpu.VMEM((T, D), jnp.bfloat16),
            pltpu.VMEM((T, D), jnp.bfloat16),
            pltpu.VMEM((unit, D), jnp.bfloat16),
            pltpu.VMEM((Z, 2 * unit, D), jnp.bfloat16),
            pltpu.VMEM((CORES, D, F), jnp.bfloat16),
            pltpu.VMEM((CORES * F, 2 * unit), jnp.bfloat16),
            pltpu.VMEM((CORES * F, D), jnp.float32),
            pltpu.VMEM((D // COLS, F, COLS), jnp.bfloat16),
            pltpu.VMEM((D // COLS, F, COLS), jnp.bfloat16),
            pltpu.VMEM((2 * unit, D), jnp.bfloat16),
            pltpu.VMEM((F, D), jnp.float32),
            pltpu.VMEM((F, D), jnp.bfloat16),
            pltpu.VMEM((F, D), jnp.bfloat16),
            pltpu.SemaphoreType.DMA((2, E)),
            pltpu.SemaphoreType.DMA((2, E)),
            pltpu.SemaphoreType.DMA((2, 2, half, 2)),
            pltpu.SemaphoreType.DMA((2, 2, half, 2)),
            pltpu.SemaphoreType.DMA((4,)),
            pltpu.SemaphoreType.DMA((4,)),
            pltpu.SemaphoreType.DMA((3, E)),
            pltpu.SemaphoreType.DMA((3, E)),
            pltpu.SemaphoreType.DMA,
            pltpu.SemaphoreType.DMA,
            pltpu.SemaphoreType.DMA((D // COLS,)),
            pltpu.SemaphoreType.DMA((D // COLS,)),
            pltpu.SemaphoreType.DMA((2,)),
            pltpu.SemaphoreType.DMA((2,)),
            pltpu.SemaphoreType.DMA((2,)),
            pltpu.SemaphoreType.DMA((2,)),
            pltpu.SemaphoreType.DMA((9,)),
            pltpu.SemaphoreType.DMA((D // COLS,)),
        ],
        compiler_params=pltpu.CompilerParams(
            collective_id=0, has_side_effects=True, vmem_limit_bytes=60 * 1024 * 1024
        ),
    )(experts.T, gate_weights.T, tokens, cotangent, w_up[0], master, moment_one, moment_two)
    return pl.pallas_call(
        functools.partial(settle, SETTLE),
        out_shape=jax.ShapeDtypeStruct((F, D), jnp.float32),
        in_specs=[anywhere],
        out_specs=anywhere,
        scratch_shapes=[
            pltpu.VMEM((F, D), jnp.float32),
            pltpu.SemaphoreType.DMA((SETTLE,)),
            pltpu.SemaphoreType.DMA((SETTLE,)),
        ],
        compiler_params=pltpu.CompilerParams(vmem_limit_bytes=60 * 1024 * 1024),
    )(fresh)[None]


def solution(mesh):
    E = mesh.shape["expert"]
    Z = mesh.shape["dp"] // (FACES * CORES)
    placed = (
        P(("expert", "dp"), None),
        P(("expert", "dp"), None),
        P(("expert", "dp"), None),
        P(("expert", "dp"), None),
        P("expert", None, "dp"),
        P(None, "dp", "expert"),
        P(None, "dp", "expert"),
        P(None, "dp", "expert"),
    )
    return jax.shard_map(
        functools.partial(body, E, Z),
        mesh=mesh,
        in_specs=placed,
        out_specs=P("expert", "dp", None),
        check_vma=False,
    )
```

```python
import functools

import jax
import jax.numpy as jnp
from jax import lax
from jax.experimental import pallas as pl
from jax.experimental.pallas import tpu as pltpu
from jax.sharding import PartitionSpec as P

CAP = 8
MESH = pl.DeviceIdType.MESH
FACES = 2
CORES = 2
NEIGHBOURS = 2
PIECE = 2 * CAP
COLS = 512
SETTLE = 8

beta_one = 0.9
beta_two = 0.95
corr_one = 1.0 - (0.9**50) ** 2
corr_two = 1.0 - (0.95**50) ** 2
learn_rate = 0.2
weight_decay = 0.1
epsilon = 1e-08


def adam_update(master, moment_one, moment_two, gradient):
    first = beta_one * moment_one.astype(jnp.float32) + (1.0 - beta_one) * gradient
    second = beta_two * moment_two.astype(jnp.float32) + (1.0 - beta_two) * gradient * gradient
    update = first / corr_one / (jnp.sqrt(second / corr_two) + epsilon)
    return master - learn_rate * (update + weight_decay * master)


def kernel(
    E,
    Z,
    experts_in,
    gates_in,
    tokens_in,
    cotangent_in,
    up_ref,
    master_ref,
    one_ref,
    two_ref,
    out_ref,
    experts_ref,
    gates_ref,
    tokens_ref,
    cotangent_ref,
    send,
    buf,
    wbuf,
    acts,
    acc,
    give,
    take,
    extra,
    far_master,
    far_one,
    far_two,
    disp_s,
    disp_r,
    ring_s,
    ring_r,
    face_s,
    face_r,
    state_s,
    state_r,
    up_s,
    up_r,
    tail_s,
    tail_r,
    share_s,
    share_r,
    early_s,
    early_r,
    local_sem,
    out_sem,
):
    e = lax.axis_index("expert")
    d = lax.axis_index("dp")
    c = lax.rem(d, CORES)
    z = lax.rem(lax.div(d, CORES), Z)
    xh = lax.div(d, CORES * Z)
    unit = E * PIECE
    part = unit // 2
    half = Z // 2
    D = tokens_ref.shape[1]
    F = up_ref.shape[1]
    width = D // E
    steps = D // COLS

    def dp_of(face, layer, core):
        return (face * Z + layer) * CORES + core

    other_face = dp_of(1 - xh, z, c)
    sibling = dp_of(xh, z, 1 - c)
    ahead = dp_of(xh, lax.rem(z + 1, Z), c)
    behind = dp_of(xh, lax.rem(z + Z - 1, Z), c)

    Y = E // NEIGHBOURS
    offsets = [(0, 0), (0, 1), (1, 0), (Y - 1, 0)]
    offsets += [(dy, dx) for dy in range(Y) for dx in range(NEIGHBOURS) if (dy, dx) not in offsets]
    near = 4

    def peer(k):
        dy, dx = offsets[k]
        y = lax.rem(lax.div(e, NEIGHBOURS) + dy, Y)
        x = lax.rem(lax.rem(e, NEIGHBOURS) + dx, NEIGHBOURS)
        return y * NEIGHBOURS + x

    barrier = pltpu.get_barrier_semaphore()
    greet = [(peer(k), d) for k in range(1, E)] + [(peer(k), other_face) for k in range(E)]
    greet += [(e, ahead), (e, behind), (e, sibling)]
    for who in greet:
        pl.semaphore_signal(barrier, inc=1, device_id=who, device_id_type=MESH)

    loads = [
        pltpu.make_async_copy(src, dst, local_sem.at[5 + i])
        for i, (src, dst) in enumerate(
            (
                (experts_in, experts_ref),
                (gates_in, gates_ref),
                (tokens_in, tokens_ref),
                (cotangent_in, cotangent_ref),
            )
        )
    ]
    for copy in loads:
        copy.start()
    own_up = pltpu.make_async_copy(up_ref, wbuf.at[c], local_sem.at[0])
    own_up.start()
    for copy in loads:
        copy.wait()

    T = tokens_ref.shape[0]
    row = lax.broadcasted_iota(jnp.int32, (unit, T), 0)
    expert_of = lax.div(row, PIECE)
    slot = lax.rem(row, PIECE)
    is_scaled = slot >= CAP
    slot = lax.rem(slot, CAP)
    first_choice = experts_ref[0:1, :] == expert_of
    second_choice = experts_ref[1:2, :] == expert_of
    named = jnp.logical_or(first_choice, second_choice)
    earlier = lax.broadcasted_iota(jnp.int32, (T, T), 0) < lax.broadcasted_iota(jnp.int32, (T, T), 1)
    place = jnp.dot(
        jnp.where(named, 1.0, 0.0).astype(jnp.bfloat16),
        jnp.where(earlier, 1.0, 0.0).astype(jnp.bfloat16),
        preferred_element_type=jnp.float32,
    )
    hit = jnp.logical_and(named, place == slot.astype(jnp.float32))
    pick_token = jnp.where(jnp.logical_and(hit, jnp.logical_not(is_scaled)), 1.0, 0.0).astype(jnp.bfloat16)
    scaled_hit = jnp.where(jnp.logical_and(hit, is_scaled), 1.0, 0.0)
    pick_scaled = scaled_hit.astype(jnp.bfloat16)
    gate = jnp.where(first_choice, gates_ref[0:1, :], 0.0) + jnp.where(second_choice, gates_ref[1:2, :], 0.0)
    gate = jnp.sum(gate * scaled_hit, axis=1, keepdims=True)

    @pl.loop(0, steps)
    def _(j):
        cols = pl.ds(pl.multiple_of(j * COLS, COLS), COLS)
        rows_token = jnp.dot(pick_token, tokens_ref[:, cols], preferred_element_type=jnp.float32)
        rows_scaled = jnp.dot(pick_scaled, cotangent_ref[:, cols], preferred_element_type=jnp.float32)
        send[:, cols] = (rows_token + rows_scaled * gate).astype(jnp.bfloat16)

    pl.semaphore_wait(barrier, len(greet))

    def piece_of(k):
        return send.at[pl.ds(pl.multiple_of(peer(k) * PIECE, PIECE), PIECE)]

    def landing(stream, k):
        return buf.at[0, pl.ds(stream * unit + k * PIECE, PIECE)]

    dispatch = {}
    for stream, where in ((0, d), (1, other_face)):
        for k in range(E):
            if stream or k:
                dispatch[stream, k] = pltpu.make_async_remote_copy(
                    src_ref=piece_of(k),
                    dst_ref=landing(stream, k),
                    send_sem=disp_s.at[stream, k],
                    recv_sem=disp_r.at[stream, k],
                    device_id=(peer(k), where),
                    device_id_type=MESH,
                )
    early = [
        pltpu.make_async_remote_copy(
            src_ref=piece_of(0),
            dst_ref=buf.at[1, pl.ds(way * unit, PIECE)],
            send_sem=early_s.at[way],
            recv_sem=early_r.at[way],
            device_id=(e, neighbour),
            device_id_type=MESH,
        )
        for way, neighbour in ((0, ahead), (1, behind))
    ]
    for copy in early:
        copy.start()
    own_piece = pltpu.make_async_copy(piece_of(0), landing(0, 0), local_sem.at[1])
    own_piece.start()
    for k in range(1, near):
        dispatch[0, k].start()
    give_up = pltpu.make_async_remote_copy(
        src_ref=up_ref,
        dst_ref=wbuf.at[c],
        send_sem=up_s,
        recv_sem=up_r,
        device_id=(e, sibling),
        device_id_type=MESH,
    )

    def lies(stream, way, s, h, skip=0, rows=None):
        if s == 0:
            b, at = 0, stream * 2 + h
        elif s == half:
            b, at = half, stream * 2 + h
        elif stream == 0:
            b, at = s, way * 2 + h
        elif s == half - 1:
            b, at = 2 * half - 1, (1 - h) * 2 + way
        else:
            b, at = half + s, way * 2 + h
        return buf.at[b, pl.ds(at * part + skip, rows or part - skip)]

    ring = {}
    for stream in range(2):
        for way, neighbour in ((0, ahead), (1, behind)):
            for s in range(half - stream):
                for h in range(2):
                    if (stream == 0 and s == half - 1 and h != way):
                        continue
                    skip = PIECE if (stream, s, h) == (0, 0, 0) else 0
                    rows = part // 2 if (stream, s, h) == (1, half - 2, 1) else None
                    ring[stream, way, s, h] = pltpu.make_async_remote_copy(
                        src_ref=lies(stream, way, s, h, skip, rows),
                        dst_ref=lies(stream, way, s + 1, h, skip, rows),
                        send_sem=ring_s.at[stream, way, s, h],
                        recv_sem=ring_r.at[stream, way, s, h],
                        device_id=(e, neighbour),
                        device_id_type=MESH,
                    )

    faces = {}
    for i, (way, s, h) in enumerate(((0, half - 1, 1), (1, half - 1, 1), (0, half, 0), (1, half, 1))):
        faces[way, s, h] = pltpu.make_async_remote_copy(
            src_ref=lies(0, way, s, h, 0 if s == half else part // 2),
            dst_ref=lies(1, way, s, h, 0 if s == half else part // 2),
            send_sem=face_s.at[i],
            recv_sem=face_r.at[i],
            device_id=(e, other_face),
            device_id_type=MESH,
        )

    def pass_on(stream, way, s, h):
        if (stream, way, s, h) in ring:
            ring[stream, way, s, h].start()
        if stream == 0 and (way, s, h) in faces:
            faces[way, s, h].start()

    def arrive(stream, s, h):
        for way in range(2):
            if (stream, way, s - 1, h) in ring:
                ring[stream, way, s - 1, h].wait_recv()
                if (stream, s, h) == (0, 1, 0):
                    early[way].wait_recv()
                pass_on(stream, way, s, h)

    own_piece.wait()
    for k in range(1, near):
        dispatch[0, k].wait_send()
    for k in range(near, E):
        dispatch[0, k].start()
    for h in range(2):
        for k in range(max(1, h * near), (h + 1) * near):
            dispatch[0, k].wait_recv()
        for way in range(2):
            pass_on(0, way, 0, h)
    give_up.start()
    for k in range(E):
        dispatch[1, k].start()

    own_cols = pl.ds(pl.multiple_of(e * width, width), width)
    state, own_state, held = [], [], []
    for k in range(1, E):
        for i, (src, dst) in enumerate(((master_ref, far_master), (one_ref, far_one), (two_ref, far_two))):
            state.append(
                pltpu.make_async_remote_copy(
                    src_ref=src.at[peer(k)],
                    dst_ref=dst.at[:, own_cols],
                    send_sem=state_s.at[i, k],
                    recv_sem=state_r.at[i, k],
                    device_id=(peer(k), d),
                    device_id_type=MESH,
                )
            )
            if i == 2 and offsets[k][1]:
                held.append(state[-1])
            else:
                state[-1].start()
    for i, (src, dst) in enumerate(((master_ref, far_master), (one_ref, far_one), (two_ref, far_two))):
        own_state.append(pltpu.make_async_copy(src.at[e], dst.at[:, own_cols], local_sem.at[2 + i]))
        own_state[-1].start()

    own_up.wait()
    give_up.wait_recv()

    def activation(rows_of, weight):
        rows = rows_of.shape[0]
        up = jnp.dot(rows_of, weight, preferred_element_type=jnp.float32)
        up = up / (1.0 + jnp.exp(-up))
        up = up.reshape(rows // PIECE, PIECE, F)[:, :CAP]
        up = jnp.concatenate([jnp.zeros_like(up), up], axis=1).reshape(rows, F)
        return up.T.astype(jnp.bfloat16)

    def hidden(b, first, rows):
        @pl.loop(0, CORES)
        def _(h):
            acts[pl.ds(pl.multiple_of(h * F, F), F), :rows] = activation(buf[b, first : first + rows], wbuf[h])

    def product(b, first, rows, cols):
        return jnp.dot(
            acts[:, :rows], buf[b, first : first + rows, cols], preferred_element_type=jnp.float32
        )

    def compute(b, first=0, rows=2 * unit, fresh=False):
        hidden(b, first, rows)

        @pl.loop(0, steps)
        def _(j):
            cols = pl.ds(pl.multiple_of(j * COLS, COLS), COLS)
            if fresh:
                acc[:, cols] = product(b, first, rows, cols)
            else:
                acc[:, cols] += product(b, first, rows, cols)

    for s in range(1, half):
        for h in range(2):
            arrive(0, s, h)
            if s == half - 1 and h == 0:
                for k in range(E):
                    dispatch[1, k].wait_recv()
                for g in range(2):
                    for way in range(2):
                        pass_on(1, way, 0, g)
        compute(s, fresh=s == 1)
    compute(0)
    for h in range(2):
        arrive(0, half, h)
    for copy in held:
        copy.start()
    for s in range(1, half - 1):
        for h in range(2):
            arrive(1, s, h)
        compute(half + s)
        if s == 1:
            compute(half, 0, unit)
    faces[0, half, 0].wait_recv()
    faces[1, half, 1].wait_recv()
    compute(half, unit, unit)

    theirs = pl.ds(pl.multiple_of((1 - c) * F, F), F)
    mine = pl.ds(pl.multiple_of(c * F, F), F)
    tail, outs = [], []
    for j in range(steps):
        give[j] = acc[theirs, pl.ds(j * COLS, COLS)].astype(jnp.bfloat16)
        tail.append(
            pltpu.make_async_remote_copy(
                src_ref=give.at[j],
                dst_ref=take.at[j],
                send_sem=tail_s.at[j],
                recv_sem=tail_r.at[j],
                device_id=(e, sibling),
                device_id_type=MESH,
            )
        )
        tail[-1].start()
    last = 2 * half - 1
    shared = [
        pltpu.make_async_remote_copy(
            src_ref=buf.at[last, pl.ds((1 - h) * unit, unit)],
            dst_ref=extra.at[pl.ds((1 - h) * unit, unit)],
            send_sem=share_s.at[h],
            recv_sem=share_r.at[h],
            device_id=(e, sibling),
            device_id_type=MESH,
        )
        for h in range(2)
    ]

    def both(h, cols):
        first = (1 - h) * unit
        own = jnp.dot(acts[:F, :unit], buf[last, first : first + unit, cols], preferred_element_type=jnp.float32)
        other = jnp.dot(acts[F:, :unit], extra[first : first + unit, cols], preferred_element_type=jnp.float32)
        return own + other

    for j in range(steps):
        tail[j].wait_recv()
        acc[mine, pl.ds(j * COLS, COLS)] += take[j].astype(jnp.float32)
    for h in range(2):
        first = (1 - h) * unit
        arrive(1, half - 1, h)
        if h:
            for way in range(2):
                faces[way, half - 1, 1].wait_recv()
        shared[h].start()
        acts[:F, :unit] = activation(buf[last, first : first + unit], wbuf[c])
        shared[h].wait_recv()
        acts[F:, :unit] = activation(extra[first : first + unit], wbuf[c])
        if h == 0:
            for j in range(steps):
                cols = pl.ds(j * COLS, COLS)
                acc[mine, cols] += both(h, cols)
            for copy in state:
                copy.wait()
            for copy in own_state:
                copy.wait()
        else:
            for j in range(steps):
                cols = pl.ds(j * COLS, COLS)
                gradient = acc[mine, cols] + both(h, cols)
                acc[mine, cols] = adam_update(far_master[:, cols], far_one[:, cols], far_two[:, cols], gradient)
                outs.append(pltpu.make_async_copy(acc.at[mine, cols], out_ref.at[:, cols], out_sem.at[j]))
                outs[-1].start()
    for k, copy in dispatch.items():
        if k[0] or k[1] >= near:
            copy.wait_send()
    for copy in [give_up] + list(ring.values()) + list(faces.values()) + tail + shared + early:
        copy.wait_send()
    for copy in outs:
        copy.wait()


def settle(pieces, src_ref, dst_ref, held, in_sems, out_sems):
    rows = src_ref.shape[0] // pieces
    coming, going = [], []
    for i in range(pieces):
        at = pl.ds(i * rows, rows)
        coming.append(pltpu.make_async_copy(src_ref.at[at], held.at[at], in_sems.at[i]))
        going.append(pltpu.make_async_copy(held.at[at], dst_ref.at[at], out_sems.at[i]))
        coming[-1].start()
    for i in range(pieces):
        coming[i].wait()
        going[i].start()
    for copy in going:
        copy.wait()


def body(E, Z, tokens, cotangent, experts, gate_weights, w_up, master, moment_one, moment_two):
    T, D = tokens.shape
    F = w_up.shape[2]
    unit = E * PIECE
    half = Z // 2
    anywhere = pl.BlockSpec(memory_space=pl.ANY)
    fresh = pl.pallas_call(
        functools.partial(kernel, E, Z),
        out_shape=jax.ShapeDtypeStruct((F, D), jnp.float32),
        in_specs=[anywhere] * 8,
        out_specs=anywhere,
        scratch_shapes=[
            pltpu.VMEM((2, T), jnp.int32),
            pltpu.VMEM((2, T), jnp.float32),
            pltpu.VMEM((T, D), jnp.bfloat16),
            pltpu.VMEM((T, D), jnp.bfloat16),
            pltpu.VMEM((unit, D), jnp.bfloat16),
            pltpu.VMEM((Z, 2 * unit, D), jnp.bfloat16),
            pltpu.VMEM((CORES, D, F), jnp.bfloat16),
            pltpu.VMEM((CORES * F, 2 * unit), jnp.bfloat16),
            pltpu.VMEM((CORES * F, D), jnp.float32),
            pltpu.VMEM((D // COLS, F, COLS), jnp.bfloat16),
            pltpu.VMEM((D // COLS, F, COLS), jnp.bfloat16),
            pltpu.VMEM((2 * unit, D), jnp.bfloat16),
            pltpu.VMEM((F, D), jnp.float32),
            pltpu.VMEM((F, D), jnp.bfloat16),
            pltpu.VMEM((F, D), jnp.bfloat16),
            pltpu.SemaphoreType.DMA((2, E)),
            pltpu.SemaphoreType.DMA((2, E)),
            pltpu.SemaphoreType.DMA((2, 2, half, 2)),
            pltpu.SemaphoreType.DMA((2, 2, half, 2)),
            pltpu.SemaphoreType.DMA((4,)),
            pltpu.SemaphoreType.DMA((4,)),
            pltpu.SemaphoreType.DMA((3, E)),
            pltpu.SemaphoreType.DMA((3, E)),
            pltpu.SemaphoreType.DMA,
            pltpu.SemaphoreType.DMA,
            pltpu.SemaphoreType.DMA((D // COLS,)),
            pltpu.SemaphoreType.DMA((D // COLS,)),
            pltpu.SemaphoreType.DMA((2,)),
            pltpu.SemaphoreType.DMA((2,)),
            pltpu.SemaphoreType.DMA((2,)),
            pltpu.SemaphoreType.DMA((2,)),
            pltpu.SemaphoreType.DMA((9,)),
            pltpu.SemaphoreType.DMA((D // COLS,)),
        ],
        compiler_params=pltpu.CompilerParams(
            collective_id=0, has_side_effects=True, vmem_limit_bytes=60 * 1024 * 1024
        ),
    )(experts.T, gate_weights.T, tokens, cotangent, w_up[0], master, moment_one, moment_two)
    return pl.pallas_call(
        functools.partial(settle, SETTLE),
        out_shape=jax.ShapeDtypeStruct((F, D), jnp.float32),
        in_specs=[anywhere],
        out_specs=anywhere,
        scratch_shapes=[
            pltpu.VMEM((F, D), jnp.float32),
            pltpu.SemaphoreType.DMA((SETTLE,)),
            pltpu.SemaphoreType.DMA((SETTLE,)),
        ],
        compiler_params=pltpu.CompilerParams(vmem_limit_bytes=60 * 1024 * 1024),
    )(fresh)[None]


def solution(mesh):
    E = mesh.shape["expert"]
    Z = mesh.shape["dp"] // (FACES * CORES)
    placed = (
        P(("expert", "dp"), None),
        P(("expert", "dp"), None),
        P(("expert", "dp"), None),
        P(("expert", "dp"), None),
        P("expert", None, "dp"),
        P(None, "dp", "expert"),
        P(None, "dp", "expert"),
        P(None, "dp", "expert"),
    )
    return jax.shard_map(
        functools.partial(body, E, Z),
        mesh=mesh,
        in_specs=placed,
        out_specs=P("expert", "dp", None),
        check_vma=False,
    )
```

```python
import functools

import jax
import jax.numpy as jnp
from jax import lax
from jax.experimental import pallas as pl
from jax.experimental.pallas import tpu as pltpu
from jax.sharding import PartitionSpec as P

CAP = 8
MESH = pl.DeviceIdType.MESH
FACES = 2
CORES = 2
NEIGHBOURS = 2
PIECE = 2 * CAP
COLS = 512
SETTLE = 8

beta_one = 0.9
beta_two = 0.95
corr_one = 1.0 - (0.9**50) ** 2
corr_two = 1.0 - (0.95**50) ** 2
learn_rate = 0.2
weight_decay = 0.1
epsilon = 1e-08


def adam_update(master, moment_one, moment_two, gradient):
    first = beta_one * moment_one.astype(jnp.float32) + (1.0 - beta_one) * gradient
    second = beta_two * moment_two.astype(jnp.float32) + (1.0 - beta_two) * gradient * gradient
    update = first / corr_one / (jnp.sqrt(second / corr_two) + epsilon)
    return master - learn_rate * (update + weight_decay * master)


def kernel(
    E,
    Z,
    experts_in,
    gates_in,
    tokens_in,
    cotangent_in,
    up_ref,
    master_ref,
    one_ref,
    two_ref,
    out_ref,
    experts_ref,
    gates_ref,
    tokens_ref,
    cotangent_ref,
    send,
    buf,
    wbuf,
    acts,
    acc,
    give,
    take,
    extra,
    far_master,
    far_one,
    far_two,
    disp_s,
    disp_r,
    ring_s,
    ring_r,
    face_s,
    face_r,
    state_s,
    state_r,
    up_s,
    up_r,
    tail_s,
    tail_r,
    share_s,
    share_r,
    early_s,
    early_r,
    local_sem,
    out_sem,
):
    e = lax.axis_index("expert")
    d = lax.axis_index("dp")
    c = lax.rem(d, CORES)
    z = lax.rem(lax.div(d, CORES), Z)
    xh = lax.div(d, CORES * Z)
    unit = E * PIECE
    part = unit // 2
    half = Z // 2
    D = tokens_ref.shape[1]
    F = up_ref.shape[1]
    width = D // E
    steps = D // COLS

    def dp_of(face, layer, core):
        return (face * Z + layer) * CORES + core

    other_face = dp_of(1 - xh, z, c)
    sibling = dp_of(xh, z, 1 - c)
    ahead = dp_of(xh, lax.rem(z + 1, Z), c)
    behind = dp_of(xh, lax.rem(z + Z - 1, Z), c)

    Y = E // NEIGHBOURS
    offsets = [(0, 0), (0, 1), (1, 0), (Y - 1, 0)]
    offsets += [(dy, dx) for dy in range(Y) for dx in range(NEIGHBOURS) if (dy, dx) not in offsets]
    near = 4

    def peer(k):
        dy, dx = offsets[k]
        y = lax.rem(lax.div(e, NEIGHBOURS) + dy, Y)
        x = lax.rem(lax.rem(e, NEIGHBOURS) + dx, NEIGHBOURS)
        return y * NEIGHBOURS + x

    barrier = pltpu.get_barrier_semaphore()
    greet = [(peer(k), d) for k in range(1, E)] + [(peer(k), other_face) for k in range(E)]
    greet += [(e, ahead), (e, behind), (e, sibling)]
    for who in greet:
        pl.semaphore_signal(barrier, inc=1, device_id=who, device_id_type=MESH)

    loads = [
        pltpu.make_async_copy(src, dst, local_sem.at[5 + i])
        for i, (src, dst) in enumerate(
            (
                (experts_in, experts_ref),
                (gates_in, gates_ref),
                (tokens_in, tokens_ref),
                (cotangent_in, cotangent_ref),
            )
        )
    ]
    for copy in loads:
        copy.start()
    own_up = pltpu.make_async_copy(up_ref, wbuf.at[c], local_sem.at[0])
    own_up.start()
    for copy in loads:
        copy.wait()

    T = tokens_ref.shape[0]
    row = lax.broadcasted_iota(jnp.int32, (unit, T), 0)
    expert_of = lax.div(row, PIECE)
    slot = lax.rem(row, PIECE)
    is_scaled = slot >= CAP
    slot = lax.rem(slot, CAP)
    first_choice = experts_ref[0:1, :] == expert_of
    second_choice = experts_ref[1:2, :] == expert_of
    named = jnp.logical_or(first_choice, second_choice)
    earlier = lax.broadcasted_iota(jnp.int32, (T, T), 0) < lax.broadcasted_iota(jnp.int32, (T, T), 1)
    place = jnp.dot(
        jnp.where(named, 1.0, 0.0).astype(jnp.bfloat16),
        jnp.where(earlier, 1.0, 0.0).astype(jnp.bfloat16),
        preferred_element_type=jnp.float32,
    )
    hit = jnp.logical_and(named, place == slot.astype(jnp.float32))
    pick_token = jnp.where(jnp.logical_and(hit, jnp.logical_not(is_scaled)), 1.0, 0.0).astype(jnp.bfloat16)
    scaled_hit = jnp.where(jnp.logical_and(hit, is_scaled), 1.0, 0.0)
    pick_scaled = scaled_hit.astype(jnp.bfloat16)
    gate = jnp.where(first_choice, gates_ref[0:1, :], 0.0) + jnp.where(second_choice, gates_ref[1:2, :], 0.0)
    gate = jnp.sum(gate * scaled_hit, axis=1, keepdims=True)

    @pl.loop(0, steps)
    def _(j):
        cols = pl.ds(pl.multiple_of(j * COLS, COLS), COLS)
        rows_token = jnp.dot(pick_token, tokens_ref[:, cols], preferred_element_type=jnp.float32)
        rows_scaled = jnp.dot(pick_scaled, cotangent_ref[:, cols], preferred_element_type=jnp.float32)
        send[:, cols] = (rows_token + rows_scaled * gate).astype(jnp.bfloat16)

    pl.semaphore_wait(barrier, len(greet))

    def piece_of(k):
        return send.at[pl.ds(pl.multiple_of(peer(k) * PIECE, PIECE), PIECE)]

    def landing(stream, k):
        return buf.at[0, pl.ds(stream * unit + k * PIECE, PIECE)]

    dispatch = {}
    for stream, where in ((0, d), (1, other_face)):
        for k in range(E):
            if stream or k:
                dispatch[stream, k] = pltpu.make_async_remote_copy(
                    src_ref=piece_of(k),
                    dst_ref=landing(stream, k),
                    send_sem=disp_s.at[stream, k],
                    recv_sem=disp_r.at[stream, k],
                    device_id=(peer(k), where),
                    device_id_type=MESH,
                )
    early = [
        pltpu.make_async_remote_copy(
            src_ref=piece_of(0),
            dst_ref=buf.at[1, pl.ds(way * unit, PIECE)],
            send_sem=early_s.at[way],
            recv_sem=early_r.at[way],
            device_id=(e, neighbour),
            device_id_type=MESH,
        )
        for way, neighbour in ((0, ahead), (1, behind))
    ]
    for copy in early:
        copy.start()
    own_piece = pltpu.make_async_copy(piece_of(0), landing(0, 0), local_sem.at[1])
    own_piece.start()
    for k in range(1, near):
        dispatch[0, k].start()
    give_up = pltpu.make_async_remote_copy(
        src_ref=up_ref,
        dst_ref=wbuf.at[c],
        send_sem=up_s,
        recv_sem=up_r,
        device_id=(e, sibling),
        device_id_type=MESH,
    )

    def lies(stream, way, s, h, skip=0, rows=None):
        if s == 0:
            b, at = 0, stream * 2 + h
        elif s == half:
            b, at = half, stream * 2 + h
        elif stream == 0:
            b, at = s, way * 2 + h
        elif s == half - 1:
            b, at = 2 * half - 1, (1 - h) * 2 + way
        else:
            b, at = half + s, way * 2 + h
        return buf.at[b, pl.ds(at * part + skip, rows or part - skip)]

    ring = {}
    for stream in range(2):
        for way, neighbour in ((0, ahead), (1, behind)):
            for s in range(half - stream):
                for h in range(2):
                    if (stream == 0 and s == half - 1 and h != way):
                        continue
                    skip = PIECE if (stream, s, h) == (0, 0, 0) else 0
                    rows = part // 2 if (stream, s, h) == (1, half - 2, 1) else None
                    ring[stream, way, s, h] = pltpu.make_async_remote_copy(
                        src_ref=lies(stream, way, s, h, skip, rows),
                        dst_ref=lies(stream, way, s + 1, h, skip, rows),
                        send_sem=ring_s.at[stream, way, s, h],
                        recv_sem=ring_r.at[stream, way, s, h],
                        device_id=(e, neighbour),
                        device_id_type=MESH,
                    )

    faces = {}
    for i, (way, s, h) in enumerate(((0, half - 1, 1), (1, half - 1, 1), (0, half, 0), (1, half, 1))):
        faces[way, s, h] = pltpu.make_async_remote_copy(
            src_ref=lies(0, way, s, h, 0 if s == half else part // 2),
            dst_ref=lies(1, way, s, h, 0 if s == half else part // 2),
            send_sem=face_s.at[i],
            recv_sem=face_r.at[i],
            device_id=(e, other_face),
            device_id_type=MESH,
        )

    def pass_on(stream, way, s, h):
        if (stream, way, s, h) in ring:
            ring[stream, way, s, h].start()
        if stream == 0 and (way, s, h) in faces:
            faces[way, s, h].start()

    def arrive(stream, s, h):
        for way in range(2):
            if (stream, way, s - 1, h) in ring:
                ring[stream, way, s - 1, h].wait_recv()
                if (stream, s, h) == (0, 1, 0):
                    early[way].wait_recv()
                pass_on(stream, way, s, h)

    own_piece.wait()
    for k in range(1, near):
        dispatch[0, k].wait_send()
    for k in range(near, E):
        dispatch[0, k].start()
    for h in range(2):
        for k in range(max(1, h * near), (h + 1) * near):
            dispatch[0, k].wait_recv()
        for way in range(2):
            pass_on(0, way, 0, h)
    give_up.start()
    for k in range(E):
        dispatch[1, k].start()

    own_cols = pl.ds(pl.multiple_of(e * width, width), width)
    state, own_state, held = [], [], []
    for k in range(1, E):
        for i, (src, dst) in enumerate(((master_ref, far_master), (one_ref, far_one), (two_ref, far_two))):
            state.append(
                pltpu.make_async_remote_copy(
                    src_ref=src.at[peer(k)],
                    dst_ref=dst.at[:, own_cols],
                    send_sem=state_s.at[i, k],
                    recv_sem=state_r.at[i, k],
                    device_id=(peer(k), d),
                    device_id_type=MESH,
                )
            )
            if i == 2 and offsets[k][1]:
                held.append(state[-1])
            else:
                state[-1].start()
    for i, (src, dst) in enumerate(((master_ref, far_master), (one_ref, far_one), (two_ref, far_two))):
        own_state.append(pltpu.make_async_copy(src.at[e], dst.at[:, own_cols], local_sem.at[2 + i]))
        own_state[-1].start()

    own_up.wait()
    give_up.wait_recv()

    def activation(rows_of, weight):
        rows = rows_of.shape[0]
        up = jnp.dot(rows_of, weight, preferred_element_type=jnp.float32)
        up = up / (1.0 + jnp.exp(-up))
        up = up.reshape(rows // PIECE, PIECE, F)[:, :CAP]
        up = jnp.concatenate([jnp.zeros_like(up), up], axis=1).reshape(rows, F)
        return up.T.astype(jnp.bfloat16)

    def hidden(b, first, rows):
        @pl.loop(0, CORES)
        def _(h):
            acts[pl.ds(pl.multiple_of(h * F, F), F), :rows] = activation(buf[b, first : first + rows], wbuf[h])

    def product(b, first, rows, cols):
        return jnp.dot(
            acts[:, :rows], buf[b, first : first + rows, cols], preferred_element_type=jnp.float32
        )

    def compute(b, first=0, rows=2 * unit, fresh=False):
        hidden(b, first, rows)

        @pl.loop(0, steps)
        def _(j):
            cols = pl.ds(pl.multiple_of(j * COLS, COLS), COLS)
            if fresh:
                acc[:, cols] = product(b, first, rows, cols)
            else:
                acc[:, cols] += product(b, first, rows, cols)

    for s in range(1, half):
        for h in range(2):
            arrive(0, s, h)
            if s == half - 1 and h == 0:
                for k in range(E):
                    dispatch[1, k].wait_recv()
                for g in range(2):
                    for way in range(2):
                        pass_on(1, way, 0, g)
        compute(s, fresh=s == 1)
    compute(0)
    arrive(0, half, 0)
    for copy in held:
        copy.start()
    arrive(0, half, 1)
    for s in range(1, half - 1):
        for h in range(2):
            arrive(1, s, h)
        compute(half + s)
        if s == 1:
            compute(half, 0, unit)
    faces[0, half, 0].wait_recv()
    faces[1, half, 1].wait_recv()
    compute(half, unit, unit)

    theirs = pl.ds(pl.multiple_of((1 - c) * F, F), F)
    mine = pl.ds(pl.multiple_of(c * F, F), F)
    tail, outs = [], []
    for j in range(steps):
        give[j] = acc[theirs, pl.ds(j * COLS, COLS)].astype(jnp.bfloat16)
        tail.append(
            pltpu.make_async_remote_copy(
                src_ref=give.at[j],
                dst_ref=take.at[j],
                send_sem=tail_s.at[j],
                recv_sem=tail_r.at[j],
                device_id=(e, sibling),
                device_id_type=MESH,
            )
        )
        tail[-1].start()
    last = 2 * half - 1
    shared = [
        pltpu.make_async_remote_copy(
            src_ref=buf.at[last, pl.ds((1 - h) * unit, unit)],
            dst_ref=extra.at[pl.ds((1 - h) * unit, unit)],
            send_sem=share_s.at[h],
            recv_sem=share_r.at[h],
            device_id=(e, sibling),
            device_id_type=MESH,
        )
        for h in range(2)
    ]

    def both(h, cols):
        first = (1 - h) * unit
        own = jnp.dot(acts[:F, :unit], buf[last, first : first + unit, cols], preferred_element_type=jnp.float32)
        other = jnp.dot(acts[F:, :unit], extra[first : first + unit, cols], preferred_element_type=jnp.float32)
        return own + other

    for j in range(steps):
        tail[j].wait_recv()
        acc[mine, pl.ds(j * COLS, COLS)] += take[j].astype(jnp.float32)
    for h in range(2):
        first = (1 - h) * unit
        arrive(1, half - 1, h)
        if h:
            for way in range(2):
                faces[way, half - 1, 1].wait_recv()
        shared[h].start()
        acts[:F, :unit] = activation(buf[last, first : first + unit], wbuf[c])
        shared[h].wait_recv()
        acts[F:, :unit] = activation(extra[first : first + unit], wbuf[c])
        if h == 0:
            for j in range(steps):
                cols = pl.ds(j * COLS, COLS)
                acc[mine, cols] += both(h, cols)
            for copy in state:
                copy.wait()
            for copy in own_state:
                copy.wait()
        else:
            for j in range(steps):
                cols = pl.ds(j * COLS, COLS)
                gradient = acc[mine, cols] + both(h, cols)
                acc[mine, cols] = adam_update(far_master[:, cols], far_one[:, cols], far_two[:, cols], gradient)
                outs.append(pltpu.make_async_copy(acc.at[mine, cols], out_ref.at[:, cols], out_sem.at[j]))
                outs[-1].start()
    for k, copy in dispatch.items():
        if k[0] or k[1] >= near:
            copy.wait_send()
    for copy in [give_up] + list(ring.values()) + list(faces.values()) + tail + shared + early:
        copy.wait_send()
    for copy in outs:
        copy.wait()


def settle(pieces, src_ref, dst_ref, held, in_sems, out_sems):
    rows = src_ref.shape[0] // pieces
    coming, going = [], []
    for i in range(pieces):
        at = pl.ds(i * rows, rows)
        coming.append(pltpu.make_async_copy(src_ref.at[at], held.at[at], in_sems.at[i]))
        going.append(pltpu.make_async_copy(held.at[at], dst_ref.at[at], out_sems.at[i]))
        coming[-1].start()
    for i in range(pieces):
        coming[i].wait()
        going[i].start()
    for copy in going:
        copy.wait()


def body(E, Z, tokens, cotangent, experts, gate_weights, w_up, master, moment_one, moment_two):
    T, D = tokens.shape
    F = w_up.shape[2]
    unit = E * PIECE
    half = Z // 2
    anywhere = pl.BlockSpec(memory_space=pl.ANY)
    fresh = pl.pallas_call(
        functools.partial(kernel, E, Z),
        out_shape=jax.ShapeDtypeStruct((F, D), jnp.float32),
        in_specs=[anywhere] * 8,
        out_specs=anywhere,
        scratch_shapes=[
            pltpu.VMEM((2, T), jnp.int32),
            pltpu.VMEM((2, T), jnp.float32),
            pltpu.VMEM((T, D), jnp.bfloat16),
            pltpu.VMEM((T, D), jnp.bfloat16),
            pltpu.VMEM((unit, D), jnp.bfloat16),
            pltpu.VMEM((Z, 2 * unit, D), jnp.bfloat16),
            pltpu.VMEM((CORES, D, F), jnp.bfloat16),
            pltpu.VMEM((CORES * F, 2 * unit), jnp.bfloat16),
            pltpu.VMEM((CORES * F, D), jnp.float32),
            pltpu.VMEM((D // COLS, F, COLS), jnp.bfloat16),
            pltpu.VMEM((D // COLS, F, COLS), jnp.bfloat16),
            pltpu.VMEM((2 * unit, D), jnp.bfloat16),
            pltpu.VMEM((F, D), jnp.float32),
            pltpu.VMEM((F, D), jnp.bfloat16),
            pltpu.VMEM((F, D), jnp.bfloat16),
            pltpu.SemaphoreType.DMA((2, E)),
            pltpu.SemaphoreType.DMA((2, E)),
            pltpu.SemaphoreType.DMA((2, 2, half, 2)),
            pltpu.SemaphoreType.DMA((2, 2, half, 2)),
            pltpu.SemaphoreType.DMA((4,)),
            pltpu.SemaphoreType.DMA((4,)),
            pltpu.SemaphoreType.DMA((3, E)),
            pltpu.SemaphoreType.DMA((3, E)),
            pltpu.SemaphoreType.DMA,
            pltpu.SemaphoreType.DMA,
            pltpu.SemaphoreType.DMA((D // COLS,)),
            pltpu.SemaphoreType.DMA((D // COLS,)),
            pltpu.SemaphoreType.DMA((2,)),
            pltpu.SemaphoreType.DMA((2,)),
            pltpu.SemaphoreType.DMA((2,)),
            pltpu.SemaphoreType.DMA((2,)),
            pltpu.SemaphoreType.DMA((9,)),
            pltpu.SemaphoreType.DMA((D // COLS,)),
        ],
        compiler_params=pltpu.CompilerParams(
            collective_id=0, has_side_effects=True, vmem_limit_bytes=60 * 1024 * 1024
        ),
    )(experts.T, gate_weights.T, tokens, cotangent, w_up[0], master, moment_one, moment_two)
    return pl.pallas_call(
        functools.partial(settle, SETTLE),
        out_shape=jax.ShapeDtypeStruct((F, D), jnp.float32),
        in_specs=[anywhere],
        out_specs=anywhere,
        scratch_shapes=[
            pltpu.VMEM((F, D), jnp.float32),
            pltpu.SemaphoreType.DMA((SETTLE,)),
            pltpu.SemaphoreType.DMA((SETTLE,)),
        ],
        compiler_params=pltpu.CompilerParams(vmem_limit_bytes=60 * 1024 * 1024),
    )(fresh)[None]


def solution(mesh):
    E = mesh.shape["expert"]
    Z = mesh.shape["dp"] // (FACES * CORES)
    placed = (
        P(("expert", "dp"), None),
        P(("expert", "dp"), None),
        P(("expert", "dp"), None),
        P(("expert", "dp"), None),
        P("expert", None, "dp"),
        P(None, "dp", "expert"),
        P(None, "dp", "expert"),
        P(None, "dp", "expert"),
    )
    return jax.shard_map(
        functools.partial(body, E, Z),
        mesh=mesh,
        in_specs=placed,
        out_specs=P("expert", "dp", None),
        check_vma=False,
    )
```
